32 devices in a mesh: energy: 4 (over y, core), slab: 8 (over z, x).
Axes of the slice: x: 2, y: 2, z: 4, core: 2. Of those that a mesh axis runs over, the one named last changes fastest.
Arguments:
- energies: float32 [8], P('energy'), may hold values from 2 to 3
- hamiltonian: bfloat16 [8, 512, 512], P('slab'), may hold values from -0.125 to 0.125
- coupling: bfloat16 [8, 512, 512], P('slab'), may hold values from -0.09375 to 0.09375
- coulomb: bfloat16 [8, 512, 512], P('slab', 'energy'), may hold values from 0.19921875 to 1
- offsets: int32 [8], replicated, may hold values from -4 to 4
Outputs:
- green: float32 [8, 8, 512, 512], P('energy', 'slab')
- self_part: bfloat16 [8, 8, 512, 512], P('energy', 'slab')
The draws below stay inside these ranges and needn't reach their ends.
All inputs are finite; a program needn't handle non-finite values.
Results may differ from the reference program's by a relative error of at most 0.0058.
Values may be sent and summed in bfloat16 or wider, within the bound.
A program may use at most 64 MiB of HBM per device.

```python
import jax
import jax.numpy as jnp
from jax import lax

K = 512
NW = 8
ROUNDS = 2
PASSES = 2
NE = 8
NB = 8


def set_ends(values, own_key, smallest, largest):
    shape = values.shape
    place = [jax.random.randint(jax.random.fold_in(own_key, axis), (), 0, shape[axis]) for axis in range(len(shape))]
    values = values.at[tuple(place)].set(smallest)
    longest = shape.index(max(shape))
    place[longest] = (place[longest] + 1) % shape[longest]
    return values.at[tuple(place)].set(largest)


def block_levels(rng, dims, split, low, top_value):
    def one(axis_at, shards_of):
        heights = jax.random.uniform(jax.random.fold_in(jax.random.fold_in(rng, 6), axis_at), (shards_of,), jnp.float32, low / len(split), top_value / len(split))
        return jnp.repeat(jnp.exp(heights), dims[axis_at] // shards_of).reshape((-1,) + (1,) * (len(dims) - axis_at - 1))

    loudness = one(*split[0])
    for cut in split[1:]:
        loudness = loudness * one(*cut)
    return loudness


def bell_draw(own_key, extent, spread, limit, split=(), kind=jnp.bfloat16):
    array = jax.random.normal(own_key, extent, jnp.float32) * spread
    if len(split) > 0:
        array = block_levels(own_key, extent, split, -0.22, 0.18) * array
    return jnp.clip(array, min=-limit, max=limit).astype(kind)


def setup_inputs(seed: int = 0) -> dict:
    key_list = jax.random.split(jax.random.key(seed), 6)
    energies = jnp.clip(2.0 + 1.0 * jax.random.uniform(key_list[0], (NE,), jnp.float32) ** block_levels(key_list[0], (NE,), ((0, 4),), -0.2, 0.2), 2.0, 3.0)
    hamiltonian = bell_draw(key_list[1], (NB, K, K), (4 * K) ** -0.5, 0.125, ((0, 8),))
    coupling = bell_draw(key_list[2], (NB, K, K), (8 * K) ** -0.5, 0.09375, ((0, 8),))
    coulomb = jnp.clip(0.19921875 + 0.80078125 * jax.random.uniform(key_list[3], (NB, K, K), jnp.float32) ** block_levels(key_list[3], (NB, K, K), ((0, 8), (1, 4)), -0.2, 0.2), 0.19921875, 1.0).astype(jnp.bfloat16)
    offsets = set_ends(jax.random.randint(key_list[4], (NW,), 0 - NE // 2, NE // 2 + 1), jax.random.fold_in(key_list[4], 1), 0 - NE // 2, (NE // 2 + 1) - 1).astype(jnp.int32)
    return {"energies": energies, "hamiltonian": hamiltonian, "coupling": coupling, "coulomb": coulomb, "offsets": offsets}


BROAD = 0.3


def unit_tables(matrix_order):
    row_index = lax.broadcasted_iota(jnp.int32, (matrix_order, matrix_order), 0)
    column_index = lax.broadcasted_iota(jnp.int32, (matrix_order, matrix_order), 1)
    half_order = matrix_order // 2
    identity = (row_index == column_index).astype(jnp.float32)
    rotate = jnp.where((row_index < half_order) & (column_index == row_index + half_order), -1.0, 0.0) + jnp.where((row_index >= half_order) & (column_index == row_index - half_order), 1.0, 0.0)
    return identity, rotate.astype(jnp.float32)


def to_bfloat(values):
    return lax.optimization_barrier(values.astype(jnp.bfloat16)).astype(jnp.float32)


def newton_step(iterate, self_part, energy, hamiltonian, coupling, identity, rotate):
    highest = lax.Precision.HIGHEST
    green_wide = iterate.astype(jnp.bfloat16).astype(jnp.float32)
    links = coupling.astype(jnp.float32)
    above_block = jnp.concatenate([green_wide[1:], jnp.zeros_like(green_wide[:1])], 0)
    right_term = to_bfloat(jnp.einsum('bij,bkj->bik', above_block, links, precision=highest))
    upper_term = jnp.einsum('bij,bjk->bik', links, right_term, precision=highest)
    inner_term = to_bfloat(jnp.einsum('bij,bjk->bik', green_wide, links, precision=highest))
    own_term = to_bfloat(jnp.einsum('bji,bjk->bik', links, inner_term, precision=highest))
    lower_term = jnp.concatenate([jnp.zeros_like(own_term[:1]), own_term[:-1]], 0)
    base_matrix = energy * identity + BROAD * rotate - hamiltonian.astype(jnp.float32)
    matrix = base_matrix - self_part.astype(jnp.float32) - upper_term - lower_term
    product = jnp.einsum('bij,bjk->bik', to_bfloat(matrix), green_wide, precision=highest)
    residue = to_bfloat(2.0 * identity - product)
    return jnp.einsum('bij,bjk->bik', green_wide, residue, precision=highest)


def pick_energies(values, positions):
    inside = (positions >= 0) & (positions < values.shape[0])
    clipped = jnp.clip(positions, 0, values.shape[0] - 1).astype(jnp.int32)
    return jnp.where(inside[:, None, None], values[clipped], 0.0)


def self_energy(green_half, coulomb, offsets):
    energy_count = green_half.shape[0]
    offset_count = offsets.shape[0]
    levels = jnp.arange(energy_count, dtype=jnp.int32)

    def per_block(packed):
        block_green, weights = packed
        values = block_green.astype(jnp.float32)
        strength = weights.astype(jnp.float32)
        running = jnp.zeros_like(values)
        for number in range(offset_count):
            offset_now = offsets[number]
            later_green = pick_energies(values, levels + offset_now)
            polarization = (4.0 / energy_count) * jnp.sum(values * later_green, axis=0)
            screened = strength * (1.0 + polarization * strength)
            running = running + screened[None] * pick_energies(values, levels - offset_now)
        return (running / offset_count).astype(jnp.bfloat16)

    result = lax.map(per_block, (jnp.moveaxis(green_half, 1, 0), coulomb))
    return jnp.moveaxis(result, 0, 1)


def reference(energies, hamiltonian, coupling, coulomb, offsets):
    energy_count = energies.shape[0]
    block_count, matrix_order = hamiltonian.shape[0], hamiltonian.shape[1]
    identity, rotate = unit_tables(matrix_order)
    green = jnp.broadcast_to(identity[None, None] / energies[:, None, None, None], (energy_count, block_count, matrix_order, matrix_order))
    self_part = jnp.zeros((energy_count, block_count, matrix_order, matrix_order), jnp.bfloat16)

    def per_energy(packed):
        return newton_step(packed[0], packed[1], packed[2], hamiltonian, coupling, identity, rotate)

    for round_index in range(ROUNDS):
        for pass_index in range(PASSES):
            green = lax.map(per_energy, (green, self_part, energies))
        self_part = self_energy(green.astype(jnp.bfloat16), coulomb, offsets)
    return green, self_part
```

```python
import functools

import jax
import jax.numpy as jnp
from jax import lax
from jax.experimental import pallas as pl
from jax.experimental.pallas import tpu as pltpu
from jax.sharding import PartitionSpec as P

ROUNDS = 2
PASSES = 2
BROAD = 0.3
BF = jnp.bfloat16
F32 = jnp.float32
MESH = pl.DeviceIdType.MESH


def dot_nn(a, b):
    return lax.dot_general(a, b, (((1,), (0,)), ((), ())), preferred_element_type=F32)


def dot_nt(a, b):
    return lax.dot_general(a, b, (((1,), (1,)), ((), ())), preferred_element_type=F32)


def kernel(
    en, inv, off, h_ref, c_ref, v_ref, go, so,
    cb, hb, cbel, ctp, ctbel, gb, gab, gbe, selfp, el, sf, gx, ret, mat, right, inner, res,
    ini_s, ini_r, hal_s, hal_r, a2a_s, a2a_r, bk_s, bk_r, gx_s, gx_r,
):
    ea, sa = lax.axis_size("energy"), lax.axis_size("slab")
    k = c_ref.shape[1]
    ne = el.shape[1]
    nw = off.shape[0]
    rc = v_ref.shape[1]
    half = k // 2
    rb = half
    me_e, me_s = lax.axis_index("energy"), lax.axis_index("slab")
    r = lax.rem(me_s, 2)
    base_s = me_s - r
    partner = base_s + 1 - r
    hh = lax.rem(me_e, 2)
    mate = me_e + 1 - 2 * hh
    flat = me_e * 2 + r
    has_above = base_s + 2 < sa
    has_below = base_s > 0
    energy = en[r]
    ge = inv[r]

    def copy(src, dst, s, q, dev):
        return pltpu.make_async_remote_copy(
            src_ref=src, dst_ref=dst, send_sem=s, recv_sem=q, device_id=dev, device_id_type=MESH
        )

    def peer(delta):
        other = lax.rem(flat + delta, ne)
        return other, other // 2, lax.rem(other, 2)

    up_dev = (me_e, me_s + 2)
    down_dev = (me_e, me_s - 2)
    barrier = pltpu.get_barrier_semaphore()
    for delta in range(1, ne):
        other, oe, orr = peer(delta)
        pl.semaphore_signal(barrier, inc=1, device_id=(oe, base_s + orr), device_id_type=MESH)

    @pl.when(has_above)
    def _():
        pl.semaphore_signal(barrier, inc=1, device_id=up_dev, device_id_type=MESH)

    @pl.when(has_below)
    def _():
        pl.semaphore_signal(barrier, inc=1, device_id=down_dev, device_id_type=MESH)

    cb[r] = c_ref[0]
    hb[r] = h_ref[0]

    @pl.when(jnp.logical_not(has_below))
    def _():
        cbel[...] = jnp.zeros_like(cbel)
        gbe[...] = jnp.zeros_like(gbe)

    @pl.when(jnp.logical_not(has_above))
    def _():
        gab[...] = jnp.zeros_like(gab)

    peers = ne - 1 + has_above.astype(jnp.int32) + has_below.astype(jnp.int32)
    pl.semaphore_wait(barrier, peers)

    mine = pl.ds(pl.multiple_of(hh * half, half), half)
    theirs = pl.ds(pl.multiple_of((1 - hh) * half, half), half)

    def pair_copy(buf, n):
        return copy(buf.at[r, mine], buf.at[r, mine], ini_s.at[n], ini_r.at[n], (me_e, partner))

    def pair_wait(buf, n):
        copy(buf.at[1 - r, mine], buf.at[1 - r, mine], ini_s.at[n], ini_r.at[n], (me_e, partner)).wait_recv()

    def mate_copy(buf, n):
        return copy(buf.at[1 - r, mine], buf.at[1 - r, mine], ini_s.at[n], ini_r.at[n], (mate, me_s))

    def mate_wait(buf, n):
        copy(buf.at[1 - r, theirs], buf.at[1 - r, theirs], ini_s.at[n], ini_r.at[n], (mate, me_s)).wait_recv()

    c1, h1 = pair_copy(cb, 0), pair_copy(hb, 1)
    c1.start()
    pair_wait(cb, 0)
    c2 = mate_copy(cb, 2)
    c2.start()
    h1.start()
    b1 = copy(cb.at[1, mine], cbel.at[mine], ini_s.at[4], ini_r.at[4], up_dev)
    b2 = copy(cbel.at[mine], cbel.at[mine], ini_s.at[5], ini_r.at[5], (mate, me_s))

    @pl.when(has_above)
    def _():
        b1.start()

    mate_wait(cb, 2)

    def rows_loop(body):
        def run(i, carry):
            i0 = pl.multiple_of(i * rb, rb)
            body(pl.ds(i0, rb), i0)
            return carry

        lax.fori_loop(0, k // rb, run, 0)

    def eye(i0):
        row = lax.broadcasted_iota(jnp.int32, (rb, k), 0) + i0
        col = lax.broadcasted_iota(jnp.int32, (rb, k), 1)
        return row, col

    def base(t, rows, i0):
        row, col = eye(i0)
        out = jnp.where(col == row, energy, 0.0)
        out = jnp.where(col == row + half, -BROAD, out)
        out = jnp.where(col == row - half, BROAD, out)
        return out - hb[t, rows].astype(F32)

    def residue(product, i0):
        row, col = eye(i0)
        return (jnp.where(col == row, 2.0, 0.0) - product).astype(BF)

    def transpose(dst, src):
        for j in range(0, k, 128):
            dst[j:j + 128, :] = src[:, j:j + 128].T

    transpose(ctp, cb[0])
    right[...] = (cb[0].astype(F32) * ge).astype(BF)
    inner[...] = (cb[1].astype(F32) * ge).astype(BF)
    keep = jnp.where(has_above, 1.0, 0.0)

    def first_local(rows, i0):
        mat[0, rows] = dot_nt(cb[0, rows], right[...])
        low = dot_nn(ctp[rows], right[...]).astype(BF).astype(F32)
        mat[1, rows] = keep * dot_nt(cb[1, rows], inner[...]) + low

    rows_loop(first_local)
    pair_wait(hb, 1)
    h2 = mate_copy(hb, 3)
    h2.start()

    @pl.when(has_below)
    def _():
        copy(cbel.at[mine], cbel.at[mine], ini_s.at[4], ini_r.at[4], down_dev).wait_recv()
        b2.start()

    mate_wait(hb, 3)

    def first_end(t, total, rows, i0):
        m = (base(t, rows, i0) - total).astype(BF).astype(F32)
        gb[0, t, rows] = (residue(m * ge, i0).astype(F32) * ge).astype(BF)

    def halo(n, slot):
        down = copy(gb.at[slot, 0], gab.at[n], hal_s.at[n, 0], hal_r.at[n, 0], down_dev)
        up = copy(gb.at[slot, 1], gbe.at[n], hal_s.at[n, 1], hal_r.at[n, 1], up_dev)
        return down, up

    def start_up(n, slot):
        @pl.when(has_above)
        def _():
            halo(n, slot)[1].start()

    def start_down(n, slot):
        @pl.when(has_below)
        def _():
            halo(n, slot)[0].start()

    rows_loop(lambda rows, i0: first_end(1, mat[1, rows], rows, i0))
    start_up(0, 0)

    @pl.when(has_below)
    def _():
        copy(cbel.at[theirs], cbel.at[theirs], ini_s.at[5], ini_r.at[5], (mate, me_s)).wait_recv()

    transpose(ctbel, cbel[...])
    right[...] = (cbel[...].astype(F32) * ge).astype(BF)

    def first_below(rows, i0):
        low = dot_nn(ctbel[rows], right[...]).astype(BF).astype(F32)
        first_end(0, mat[0, rows] + low, rows, i0)

    rows_loop(first_below)
    start_down(0, 0)

    def newton(n, use_self, last, send_next):
        def local_a(rows, i0):
            right[rows] = dot_nt(gb[n, 1, rows], cb[0]).astype(BF)
            inner[rows] = dot_nn(gb[n, 0, rows], cb[0]).astype(BF)

        rows_loop(local_a)

        def local_b(rows, i0):
            up = base(0, rows, i0) - dot_nn(cb[0, rows], right[...])
            low = base(1, rows, i0) - dot_nn(ctp[rows], inner[...]).astype(BF).astype(F32)
            if use_self:
                up = up - selfp[0, rows].astype(F32)
                low = low - selfp[1, rows].astype(F32)
            mat[0, rows] = up
            mat[1, rows] = low

        rows_loop(local_b)

        def finish(t, remote):
            def product(rows, i0):
                m = (mat[t, rows] - remote(rows)).astype(BF)
                res[rows] = residue(dot_nn(m, gb[n, t]), i0)

            rows_loop(product)

            def green(rows, i0):
                value = dot_nn(gb[n, t, rows], res[...])
                gb[n + 1, t, rows] = value.astype(BF)
                if last:
                    @pl.when(r == t)
                    def _():
                        go[t, 0, rows] = value

            rows_loop(green)

        @pl.when(has_above)
        def _():
            copy(gab.at[n], gab.at[n], hal_s.at[n, 0], hal_r.at[n, 0], up_dev).wait_recv()

        def remote_a(rows, i0):
            right[rows] = dot_nt(gab[n, rows], cb[1]).astype(BF)

        rows_loop(remote_a)
        finish(1, lambda rows: dot_nn(cb[1, rows], right[...]))
        if send_next:
            start_up(n + 1, n + 1)

        @pl.when(has_below)
        def _():
            copy(gbe.at[n], gbe.at[n], hal_s.at[n, 1], hal_r.at[n, 1], down_dev).wait_recv()

        def remote_b(rows, i0):
            inner[rows] = dot_nn(gbe[n, rows], cbel[...]).astype(BF)

        rows_loop(remote_b)
        finish(0, lambda rows: dot_nn(ctbel[rows], inner[...]).astype(BF).astype(F32))
        if send_next:
            start_down(n + 1, n + 1)

    def count(d):
        total = jnp.float32(0.0)
        for j in range(nw):
            total = total + jnp.where(off[j] == d, 1.0 / nw, 0.0)
        return total

    myrows = pl.ds(pl.multiple_of(me_e * rc, rc), rc)

    def scatter(rd, slot, delta):
        other, oe, orr = peer(delta)
        rows = pl.ds(pl.multiple_of(oe * rc, rc), rc)
        return copy(
            gb.at[slot, orr, rows], el.at[rd, flat], a2a_s.at[rd, other], a2a_r.at[rd, flat],
            (oe, base_s + orr),
        )

    def gather_wait(rd, delta):
        other, oe, orr = peer(delta)
        copy(
            el.at[rd, other], el.at[rd, other], a2a_s.at[rd, other], a2a_r.at[rd, other],
            (oe, base_s + orr),
        ).wait_recv()

    def convolve(rd, slot):
        for delta in range(1, ne):
            scatter(rd, slot, delta).start()
        el[rd, flat] = gb[slot, r, myrows]

        def after():
            for delta in range(1, ne):
                gather_wait(rd, delta)
            top = ne // 2
            ahead = [count(d) for d in range(top + 1)]
            behind = [count(-d) for d in range(top + 1)]
            columns = k // 128

            def tile(i, carry):
                rows = pl.ds(pl.multiple_of((i // columns) * 16, 16), 16)
                cols = pl.ds(pl.multiple_of(lax.rem(i, columns) * 128, 128), 128)
                g = [el[rd, e, rows, cols].astype(F32) for e in range(ne)]
                v = v_ref[0, rows, cols].astype(F32)
                acc = [jnp.zeros((16, 128), F32) for _ in range(ne)]
                for d in range(top + 1):
                    pol = g[0] * g[d]
                    for e in range(1, ne - d):
                        pol = pol + g[e] * g[e + d]
                    scr = v * (1.0 + (4.0 / ne) * pol * v)
                    a = scr * ahead[d]
                    b = scr * behind[d]
                    for e in range(ne):
                        if e - d >= 0:
                            acc[e] = acc[e] + a * g[e - d]
                        if d > 0 and e + d < ne:
                            acc[e] = acc[e] + b * g[e + d]
                for e in range(ne):
                    sf[rd, e, rows, cols] = acc[e].astype(BF)
                return carry

            lax.fori_loop(0, (rc // 16) * columns, tile, 0)

        return after

    newton(0, False, False, False)
    convolve(0, 1)()

    def back(delta):
        other, oe, orr = peer(delta)
        return copy(
            sf.at[0, other], selfp.at[r, myrows], bk_s.at[0, other], bk_r.at[0, flat],
            (oe, base_s + orr),
        )

    start_up(1, 1)
    start_down(1, 1)
    for delta in range(1, ne):
        back(delta).start()
    selfp[r, myrows] = sf[0, flat]
    for delta in range(1, ne):
        other, oe, orr = peer(delta)
        rows = pl.ds(pl.multiple_of(oe * rc, rc), rc)
        copy(
            sf.at[0, other], selfp.at[orr, rows], bk_s.at[0, other], bk_r.at[0, other],
            (oe, base_s + orr),
        ).wait_recv()

    newton(1, True, False, True)
    newton(2, True, True, False)
    finish_last = convolve(1, 3)
    cross = copy(gb.at[3, 1 - r], gx, gx_s, gx_r, (me_e, partner))
    cross.start()
    finish_last()

    def home(delta):
        oe = lax.rem(me_e + delta, ea)
        return copy(
            sf.at[1, pl.ds(oe * 2, 2)], ret.at[:, myrows], bk_s.at[1, oe], bk_r.at[1, me_e],
            (oe, me_s),
        )

    for delta in range(1, ea):
        home(delta).start()
    ret[:, myrows] = sf[1, pl.ds(me_e * 2, 2)]
    cross.wait_recv()

    def widen(rows, i0):
        go[1 - r, 0, rows] = gx[rows].astype(F32)

    rows_loop(widen)
    for delta in range(1, ea):
        oe = lax.rem(me_e + delta, ea)
        rows = pl.ds(pl.multiple_of(oe * rc, rc), rc)
        copy(
            sf.at[1, pl.ds(oe * 2, 2)], ret.at[:, rows], bk_s.at[1, oe], bk_r.at[1, oe], (oe, me_s)
        ).wait_recv()
    so[:, 0] = ret[...]

    for c in (c1, h1, c2, h2, cross):
        c.wait_send()

    @pl.when(has_above)
    def _():
        b1.wait_send()
        for n in range(3):
            halo(n, n)[1].wait_send()

    @pl.when(has_below)
    def _():
        b2.wait_send()
        for n in range(3):
            halo(n, n)[0].wait_send()

    for delta in range(1, ne):
        scatter(0, 1, delta).wait_send()
        scatter(1, 3, delta).wait_send()
        back(delta).wait_send()
    for delta in range(1, ea):
        home(delta).wait_send()


def local(energies, hamiltonian, coupling, coulomb, offsets):
    k = hamiltonian.shape[1]
    rc = coulomb.shape[1]
    ne = energies.shape[0] * lax.axis_size("energy")
    inverse = lax.reduce_precision(1.0 / energies, 8, 7)
    smem = pl.BlockSpec(memory_space=pltpu.SMEM)
    vmem = pl.BlockSpec(memory_space=pltpu.VMEM)
    dma = pltpu.SemaphoreType.DMA

    def buf(*shape, kind=BF):
        return pltpu.VMEM(shape, kind)

    return pl.pallas_call(
        kernel,
        out_shape=(
            jax.ShapeDtypeStruct((2, 1, k, k), F32),
            jax.ShapeDtypeStruct((2, 1, k, k), BF),
        ),
        in_specs=[smem, smem, smem, vmem, vmem, vmem],
        out_specs=(vmem, vmem),
        scratch_shapes=[
            buf(2, k, k), buf(2, k, k), buf(k, k), buf(k, k), buf(k, k),
            buf(4, 2, k, k), buf(3, k, k), buf(3, k, k), buf(2, k, k),
            buf(2, ne, rc, k), buf(2, ne, rc, k), buf(k, k), buf(2, k, k),
            buf(2, k, k, kind=F32), buf(k, k), buf(k, k), buf(k, k),
            dma((6,)), dma((6,)), dma((3, 2)), dma((3, 2)),
            dma((2, ne)), dma((2, ne)), dma((2, ne)), dma((2, ne)), dma, dma,
        ],
        compiler_params=pltpu.CompilerParams(
            collective_id=0, has_side_effects=True, vmem_limit_bytes=48 * 1024 * 1024
        ),
    )(energies, inverse, offsets, hamiltonian, coupling, coulomb)


def solution(mesh):
    placed = (
        P("energy"),
        P("slab", None, None),
        P("slab", None, None),
        P("slab", "energy", None),
        P(),
    )
    return jax.shard_map(
        local,
        mesh=mesh,
        in_specs=placed,
        out_specs=(P("energy", "slab", None, None), P("energy", "slab", None, None)),
        check_vma=False,
    )
```

```python
import functools

import jax
import jax.numpy as jnp
from jax import lax
from jax.experimental import pallas as pl
from jax.experimental.pallas import tpu as pltpu
from jax.sharding import PartitionSpec as P

ROUNDS = 2
PASSES = 2
BROAD = 0.3
BF = jnp.bfloat16
F32 = jnp.float32
MESH = pl.DeviceIdType.MESH


def dot_nn(a, b):
    return lax.dot_general(a, b, (((1,), (0,)), ((), ())), preferred_element_type=F32)


def dot_nt(a, b):
    return lax.dot_general(a, b, (((1,), (1,)), ((), ())), preferred_element_type=F32)


def kernel(
    nw, pack, h_ref, c_ref, v_ref, go, so,
    cb, hb, cbel, ctp, ctbel, gb, gab, gbe, selfp, el, sf, gx, ret, mat, right, inner, res,
    vb, loc, ini_s, ini_r, hal_s, hal_r, a2a_s, a2a_r, bk_s, bk_r, gx_s, gx_r,
):
    ea, sa = lax.axis_size("energy"), lax.axis_size("slab")
    k = c_ref.shape[1]
    ne = el.shape[1]
    rc = v_ref.shape[1]
    half = k // 2
    rb = half
    me_e, me_s = lax.axis_index("energy"), lax.axis_index("slab")
    r = lax.rem(me_s, 2)
    base_s = me_s - r
    partner = base_s + 1 - r
    hh = lax.rem(me_e, 2)
    mate = me_e + 1 - 2 * hh
    flat = me_e * 2 + r
    has_above = base_s + 2 < sa
    has_below = base_s > 0
    energy = pack[r]
    ge = pack[2 + r]

    def copy(src, dst, s, q, dev):
        return pltpu.make_async_remote_copy(
            src_ref=src, dst_ref=dst, send_sem=s, recv_sem=q, device_id=dev, device_id_type=MESH
        )

    def peer(delta):
        other = lax.rem(flat + delta, ne)
        return other, other // 2, lax.rem(other, 2)

    up_dev = (me_e, me_s + 2)
    down_dev = (me_e, me_s - 2)
    barrier = pltpu.get_barrier_semaphore()
    for delta in range(1, ne):
        other, oe, orr = peer(delta)
        pl.semaphore_signal(barrier, inc=1, device_id=(oe, base_s + orr), device_id_type=MESH)

    @pl.when(has_above)
    def _():
        pl.semaphore_signal(barrier, inc=1, device_id=up_dev, device_id_type=MESH)

    @pl.when(has_below)
    def _():
        pl.semaphore_signal(barrier, inc=1, device_id=down_dev, device_id_type=MESH)

    own_c = pltpu.make_async_copy(c_ref.at[0], cb.at[r], loc.at[0])
    own_h = pltpu.make_async_copy(h_ref.at[0], hb.at[r], loc.at[1])
    own_v = pltpu.make_async_copy(v_ref.at[0], vb, loc.at[2])
    own_c.start()
    own_h.start()
    own_v.start()

    @pl.when(jnp.logical_not(has_below))
    def _():
        cbel[...] = jnp.zeros_like(cbel)
        gbe[...] = jnp.zeros_like(gbe)

    @pl.when(jnp.logical_not(has_above))
    def _():
        gab[...] = jnp.zeros_like(gab)

    peers = ne - 1 + has_above.astype(jnp.int32) + has_below.astype(jnp.int32)
    pl.semaphore_wait(barrier, peers)

    mine = pl.ds(pl.multiple_of(hh * half, half), half)
    theirs = pl.ds(pl.multiple_of((1 - hh) * half, half), half)

    def pair_copy(src, buf, n):
        return copy(src.at[0, mine], buf.at[r, mine], ini_s.at[n], ini_r.at[n], (me_e, partner))

    def pair_wait(buf, n):
        copy(buf.at[1 - r, mine], buf.at[1 - r, mine], ini_s.at[n], ini_r.at[n], (me_e, partner)).wait_recv()

    def mate_copy(buf, n):
        return copy(buf.at[1 - r, mine], buf.at[1 - r, mine], ini_s.at[n], ini_r.at[n], (mate, me_s))

    def mate_wait(buf, n):
        copy(buf.at[1 - r, theirs], buf.at[1 - r, theirs], ini_s.at[n], ini_r.at[n], (mate, me_s)).wait_recv()

    c1, h1 = pair_copy(c_ref, cb, 0), pair_copy(h_ref, hb, 1)
    c1.start()
    b0 = copy(c_ref.at[0, mine], cbel.at[mine], ini_s.at[4], ini_r.at[4], up_dev)
    b1 = copy(cb.at[1, mine], cbel.at[mine], ini_s.at[4], ini_r.at[4], up_dev)
    b2 = copy(cbel.at[mine], cbel.at[mine], ini_s.at[5], ini_r.at[5], (mate, me_s))

    @pl.when(jnp.logical_and(has_above, r == 1))
    def _():
        b0.start()

    pair_wait(cb, 0)
    c2 = mate_copy(cb, 2)
    c2.start()
    h1.start()

    @pl.when(jnp.logical_and(has_above, r == 0))
    def _():
        b1.start()

    own_c.wait()
    mate_wait(cb, 2)

    def rows_loop(body):
        def run(i, carry):
            i0 = pl.multiple_of(i * rb, rb)
            body(pl.ds(i0, rb), i0)
            return carry

        lax.fori_loop(0, k // rb, run, 0)

    def eye(i0):
        row = lax.broadcasted_iota(jnp.int32, (rb, k), 0) + i0
        col = lax.broadcasted_iota(jnp.int32, (rb, k), 1)
        return row, col

    def base(t, rows, i0):
        row, col = eye(i0)
        out = jnp.where(col == row, energy, 0.0)
        out = jnp.where(col == row + half, -BROAD, out)
        out = jnp.where(col == row - half, BROAD, out)
        return out - hb[t, rows].astype(F32)

    def residue(product, i0):
        row, col = eye(i0)
        return (jnp.where(col == row, 2.0, 0.0) - product).astype(BF)

    def transpose(dst, src):
        for j in range(0, k, 128):
            dst[j:j + 128, :] = src[:, j:j + 128].T

    transpose(ctp, cb[0])
    right[...] = (cb[0].astype(F32) * ge).astype(BF)
    inner[...] = (cb[1].astype(F32) * ge).astype(BF)
    keep = jnp.where(has_above, 1.0, 0.0)

    def first_local(rows, i0):
        mat[0, rows] = dot_nt(cb[0, rows], right[...])
        low = dot_nn(ctp[rows], right[...]).astype(BF).astype(F32)
        mat[1, rows] = keep * dot_nt(cb[1, rows], inner[...]) + low

    rows_loop(first_local)
    pair_wait(hb, 1)
    h2 = mate_copy(hb, 3)
    h2.start()

    @pl.when(has_below)
    def _():
        copy(cbel.at[mine], cbel.at[mine], ini_s.at[4], ini_r.at[4], down_dev).wait_recv()
        b2.start()

    mate_wait(hb, 3)
    own_h.wait()

    def first_end(t, total, rows, i0):
        m = (base(t, rows, i0) - total).astype(BF).astype(F32)
        gb[0, t, rows] = (residue(m * ge, i0).astype(F32) * ge).astype(BF)

    def halo(n, slot):
        down = copy(gb.at[slot, 0], gab.at[n], hal_s.at[n, 0], hal_r.at[n, 0], down_dev)
        up = copy(gb.at[slot, 1], gbe.at[n], hal_s.at[n, 1], hal_r.at[n, 1], up_dev)
        return down, up

    def start_up(n, slot):
        @pl.when(has_above)
        def _():
            halo(n, slot)[1].start()

    def start_down(n, slot):
        @pl.when(has_below)
        def _():
            halo(n, slot)[0].start()

    rows_loop(lambda rows, i0: first_end(1, mat[1, rows], rows, i0))
    start_up(0, 0)

    @pl.when(has_below)
    def _():
        copy(cbel.at[theirs], cbel.at[theirs], ini_s.at[5], ini_r.at[5], (mate, me_s)).wait_recv()

    transpose(ctbel, cbel[...])
    right[...] = (cbel[...].astype(F32) * ge).astype(BF)

    def first_below(rows, i0):
        low = dot_nn(ctbel[rows], right[...]).astype(BF).astype(F32)
        first_end(0, mat[0, rows] + low, rows, i0)

    rows_loop(first_below)
    start_down(0, 0)

    def local_part(n):
        def local_a(rows, i0):
            right[rows] = dot_nt(gb[n, 1, rows], cb[0]).astype(BF)
            inner[rows] = dot_nn(gb[n, 0, rows], cb[0]).astype(BF)

        rows_loop(local_a)

        def local_b(rows, i0):
            mat[0, rows] = base(0, rows, i0) - dot_nn(cb[0, rows], right[...])
            low = dot_nn(ctp[rows], inner[...]).astype(BF).astype(F32)
            mat[1, rows] = base(1, rows, i0) - low

        rows_loop(local_b)

    def remote_part(n, t):
        if t == 1:
            @pl.when(has_above)
            def _():
                copy(gab.at[n], gab.at[n], hal_s.at[n, 0], hal_r.at[n, 0], up_dev).wait_recv()

            def remote_a(rows, i0):
                right[rows] = dot_nt(gab[n, rows], cb[1]).astype(BF)

            rows_loop(remote_a)
            return lambda rows: dot_nn(cb[1, rows], right[...])

        @pl.when(has_below)
        def _():
            copy(gbe.at[n], gbe.at[n], hal_s.at[n, 1], hal_r.at[n, 1], down_dev).wait_recv()

        def remote_b(rows, i0):
            inner[rows] = dot_nn(gbe[n, rows], cbel[...]).astype(BF)

        rows_loop(remote_b)
        return lambda rows: dot_nn(ctbel[rows], inner[...]).astype(BF).astype(F32)

    def finish(n, t, term, last):
        def product(rows, i0):
            m = (mat[t, rows] - term(rows)).astype(BF)
            res[rows] = residue(dot_nn(m, gb[n, t]), i0)

        rows_loop(product)

        def green(rows, i0):
            value = dot_nn(gb[n, t, rows], res[...])
            gb[n + 1, t, rows] = value.astype(BF)
            if last:
                @pl.when(r == t)
                def _():
                    go[t, 0, rows] = value

        rows_loop(green)

    def start_halo(n, t):
        (start_up if t else start_down)(n, n)

    def self_term(t):
        return lambda rows: selfp[t, rows].astype(F32)

    def count(d):
        total = jnp.float32(0.0)
        for j in range(nw):
            total = total + jnp.where(pack[4 + j] == d, 1.0 / nw, 0.0)
        return total

    myrows = pl.ds(pl.multiple_of(me_e * rc, rc), rc)

    def scatter(rd, slot, t, method):
        for delta in range(ea):
            oe = lax.rem(me_e + delta, ea)
            rows = pl.ds(pl.multiple_of(oe * rc, rc), rc)
            piece = copy(
                gb.at[slot, t, rows], el.at[rd, flat], a2a_s.at[rd, oe * 2 + t], a2a_r.at[rd, flat],
                (oe, base_s + t),
            )
            if delta == 0:
                pl.when(r != t)(getattr(piece, method))
            else:
                getattr(piece, method)()

    def gather_wait(rd, delta):
        other, oe, orr = peer(delta)
        copy(
            el.at[rd, other], el.at[rd, other], a2a_s.at[rd, other], a2a_r.at[rd, other],
            (oe, base_s + orr),
        ).wait_recv()

    def convolve(rd):
        top = ne // 2
        ahead = [count(d) for d in range(top + 1)]
        behind = [count(-d) for d in range(top + 1)]
        columns = k // 128

        def tile(i, carry):
            rows = pl.ds(pl.multiple_of((i // columns) * 16, 16), 16)
            cols = pl.ds(pl.multiple_of(lax.rem(i, columns) * 128, 128), 128)
            g = [el[rd, e, rows, cols].astype(F32) for e in range(ne)]
            v = vb[rows, cols].astype(F32)
            acc = [jnp.zeros((16, 128), F32) for _ in range(ne)]
            for d in range(top + 1):
                pol = g[0] * g[d]
                for e in range(1, ne - d):
                    pol = pol + g[e] * g[e + d]
                scr = v * (1.0 + (4.0 / ne) * pol * v)
                a = scr * ahead[d]
                b = scr * behind[d]
                for e in range(ne):
                    if e - d >= 0:
                        acc[e] = acc[e] + a * g[e - d]
                    if d > 0 and e + d < ne:
                        acc[e] = acc[e] + b * g[e + d]
            for e in range(ne):
                sf[rd, e, rows, cols] = acc[e].astype(BF)
            return carry

        lax.fori_loop(0, (rc // 16) * columns, tile, 0)

    def gather_all(rd):
        for delta in range(1, ne):
            gather_wait(rd, delta)

    local_part(0)
    for t in (0, 1):
        finish(0, t, remote_part(0, t), False)
        scatter(0, 1, t, "start")
        start_halo(1, t)
    el[0, flat] = gb[1, r, myrows]
    local_part(1)
    own_v.wait()
    gather_all(0)
    convolve(0)

    def back(delta):
        other, oe, orr = peer(delta)
        return copy(
            sf.at[0, other], selfp.at[r, myrows], bk_s.at[0, other], bk_r.at[0, flat],
            (oe, base_s + orr),
        )

    for delta in range(1, ne):
        back(delta).start()
    selfp[r, myrows] = sf[0, flat]
    for t in (0, 1):
        term = remote_part(1, t)

        def add(rows, i0, t=t, term=term):
            mat[t, rows] = mat[t, rows] - term(rows)

        rows_loop(add)
    for delta in range(1, ne):
        other, oe, orr = peer(delta)
        rows = pl.ds(pl.multiple_of(oe * rc, rc), rc)
        copy(
            sf.at[0, other], selfp.at[orr, rows], bk_s.at[0, other], bk_r.at[0, other],
            (oe, base_s + orr),
        ).wait_recv()

    for t in (1, 0):
        finish(1, t, self_term(t), False)
        start_halo(2, t)
    local_part(2)
    for t in (0, 1):
        term = remote_part(2, t)

        def whole(rows, t=t, term=term):
            return selfp[t, rows].astype(F32) + term(rows)

        finish(2, t, whole, True)
        scatter(1, 3, t, "start")
    el[1, flat] = gb[3, r, myrows]
    cross = copy(gb.at[3, 1 - r], gx, gx_s, gx_r, (me_e, partner))
    gather_all(1)
    cross.start()
    convolve(1)

    def home(delta):
        oe = lax.rem(me_e + delta, ea)
        return copy(
            sf.at[1, pl.ds(oe * 2, 2)], ret.at[:, myrows], bk_s.at[1, oe], bk_r.at[1, me_e],
            (oe, me_s),
        )

    for delta in range(1, ea):
        home(delta).start()
    ret[:, myrows] = sf[1, pl.ds(me_e * 2, 2)]
    cross.wait_recv()

    def widen(rows, i0):
        go[1 - r, 0, rows] = gx[rows].astype(F32)

    rows_loop(widen)
    for delta in range(1, ea):
        oe = lax.rem(me_e + delta, ea)
        rows = pl.ds(pl.multiple_of(oe * rc, rc), rc)
        copy(
            sf.at[1, pl.ds(oe * 2, 2)], ret.at[:, rows], bk_s.at[1, oe], bk_r.at[1, oe], (oe, me_s)
        ).wait_recv()
    so[:, 0] = ret[...]

    for c in (c1, h1, c2, h2, cross):
        c.wait_send()

    @pl.when(has_above)
    def _():
        b1.wait_send()
        for n in range(3):
            halo(n, n)[1].wait_send()

    @pl.when(has_below)
    def _():
        b2.wait_send()
        for n in range(3):
            halo(n, n)[0].wait_send()

    for delta in range(1, ne):
        back(delta).wait_send()
    for t in (0, 1):
        scatter(0, 1, t, "wait_send")
        scatter(1, 3, t, "wait_send")
    for delta in range(1, ea):
        home(delta).wait_send()


def local(energies, hamiltonian, coupling, coulomb, offsets):
    k = hamiltonian.shape[1]
    rc = coulomb.shape[1]
    ne = energies.shape[0] * lax.axis_size("energy")
    inverse = lax.reduce_precision(1.0 / energies, 8, 7)
    pack = jnp.concatenate([energies, inverse, offsets.astype(F32)])
    hbm = pl.BlockSpec(memory_space=pltpu.HBM)
    smem = pl.BlockSpec(memory_space=pltpu.SMEM)
    vmem = pl.BlockSpec(memory_space=pltpu.VMEM)
    dma = pltpu.SemaphoreType.DMA

    def buf(*shape, kind=BF):
        return pltpu.VMEM(shape, kind)

    return pl.pallas_call(
        functools.partial(kernel, offsets.shape[0]),
        out_shape=(
            jax.ShapeDtypeStruct((2, 1, k, k), F32),
            jax.ShapeDtypeStruct((2, 1, k, k), BF),
        ),
        in_specs=[smem, hbm, hbm, hbm],
        out_specs=(vmem, vmem),
        scratch_shapes=[
            buf(2, k, k), buf(2, k, k), buf(k, k), buf(k, k), buf(k, k),
            buf(4, 2, k, k), buf(3, k, k), buf(3, k, k), buf(2, k, k),
            buf(2, ne, rc, k), buf(2, ne, rc, k), buf(k, k), buf(2, k, k),
            buf(2, k, k, kind=F32), buf(k, k), buf(k, k), buf(k, k),
            buf(rc, k), dma((3,)),
            dma((6,)), dma((6,)), dma((3, 2)), dma((3, 2)),
            dma((2, ne)), dma((2, ne)), dma((2, ne)), dma((2, ne)), dma, dma,
        ],
        compiler_params=pltpu.CompilerParams(
            collective_id=0, has_side_effects=True, vmem_limit_bytes=48 * 1024 * 1024
        ),
    )(pack, hamiltonian, coupling, coulomb)


def solution(mesh):
    placed = (
        P("energy"),
        P("slab", None, None),
        P("slab", None, None),
        P("slab", "energy", None),
        P(),
    )
    return jax.shard_map(
        local,
        mesh=mesh,
        in_specs=placed,
        out_specs=(P("energy", "slab", None, None), P("energy", "slab", None, None)),
        check_vma=False,
    )
```

```python
import jax
import jax.numpy as jnp
from jax import lax
from jax.experimental import pallas as pl
from jax.experimental.pallas import tpu as pltpu
from jax.sharding import PartitionSpec as P

ROUNDS = 2
PASSES = 2
BROAD = 0.3
BF = jnp.bfloat16
F32 = jnp.float32
MESH = pl.DeviceIdType.MESH


def dot_nn(a, b):
    return lax.dot_general(a, b, (((1,), (0,)), ((), ())), preferred_element_type=F32)


def dot_nt(a, b):
    return lax.dot_general(a, b, (((1,), (1,)), ((), ())), preferred_element_type=F32)


def kernel(
    en, off, h_ref, c_ref, v_ref, go, so,
    cb, hb, cbel, ctp, ctbel, gb, gab, gbe, selfp, el, sf, gx, ret, mat, right, inner, res,
    vb, loc, ini_s, ini_r, hal_s, hal_r, a2a_s, a2a_r, bk_s, bk_r, gx_s, gx_r,
):
    ea, sa = lax.axis_size("energy"), lax.axis_size("slab")
    k = c_ref.shape[1]
    ne = el.shape[1]
    rc = v_ref.shape[1]
    half = k // 2
    rb = k
    me_e, me_s = lax.axis_index("energy"), lax.axis_index("slab")
    r = lax.rem(me_s, 2)
    base_s = me_s - r
    partner = base_s + 1 - r
    hh = lax.rem(me_e, 2)
    mate = me_e + 1 - 2 * hh
    flat = me_e * 2 + r
    has_above = base_s + 2 < sa
    has_below = base_s > 0
    nw = off.shape[0]
    energy = en[r]
    ge = (1.0 / jnp.full((1, k), energy, F32)).astype(BF).astype(F32)

    def copy(src, dst, s, q, dev):
        return pltpu.make_async_remote_copy(
            src_ref=src, dst_ref=dst, send_sem=s, recv_sem=q, device_id=dev, device_id_type=MESH
        )

    def peer(delta):
        other = lax.rem(flat + delta, ne)
        return other, other // 2, lax.rem(other, 2)

    up_dev = (me_e, me_s + 2)
    down_dev = (me_e, me_s - 2)
    barrier = pltpu.get_barrier_semaphore()
    for delta in range(1, ne):
        other, oe, orr = peer(delta)
        pl.semaphore_signal(barrier, inc=1, device_id=(oe, base_s + orr), device_id_type=MESH)

    @pl.when(has_above)
    def _():
        pl.semaphore_signal(barrier, inc=1, device_id=up_dev, device_id_type=MESH)

    @pl.when(has_below)
    def _():
        pl.semaphore_signal(barrier, inc=1, device_id=down_dev, device_id_type=MESH)

    own_c = pltpu.make_async_copy(c_ref.at[0], cb.at[r], loc.at[0])
    own_h = pltpu.make_async_copy(h_ref.at[0], hb.at[r], loc.at[1])
    own_v = pltpu.make_async_copy(v_ref.at[0], vb, loc.at[2])
    own_c.start()
    own_h.start()
    own_v.start()

    @pl.when(jnp.logical_not(has_below))
    def _():
        cbel[...] = jnp.zeros_like(cbel)
        gbe[...] = jnp.zeros_like(gbe)

    @pl.when(jnp.logical_not(has_above))
    def _():
        gab[...] = jnp.zeros_like(gab)

    peers = ne - 1 + has_above.astype(jnp.int32) + has_below.astype(jnp.int32)
    pl.semaphore_wait(barrier, peers)

    mine = pl.ds(pl.multiple_of(hh * half, half), half)
    theirs = pl.ds(pl.multiple_of((1 - hh) * half, half), half)

    def pair_copy(src, buf, n):
        return copy(src.at[0, mine], buf.at[r, mine], ini_s.at[n], ini_r.at[n], (me_e, partner))

    def pair_wait(buf, n):
        copy(buf.at[1 - r, mine], buf.at[1 - r, mine], ini_s.at[n], ini_r.at[n], (me_e, partner)).wait_recv()

    def mate_copy(buf, n):
        return copy(buf.at[1 - r, mine], buf.at[1 - r, mine], ini_s.at[n], ini_r.at[n], (mate, me_s))

    def mate_wait(buf, n):
        copy(buf.at[1 - r, theirs], buf.at[1 - r, theirs], ini_s.at[n], ini_r.at[n], (mate, me_s)).wait_recv()

    c1, h1 = pair_copy(c_ref, cb, 0), pair_copy(h_ref, hb, 1)
    c1.start()
    b0 = copy(c_ref.at[0, mine], cbel.at[mine], ini_s.at[4], ini_r.at[4], up_dev)
    b1 = copy(cb.at[1, mine], cbel.at[mine], ini_s.at[4], ini_r.at[4], up_dev)
    b2 = copy(cbel.at[mine], cbel.at[mine], ini_s.at[5], ini_r.at[5], (mate, me_s))

    @pl.when(jnp.logical_and(has_above, r == 1))
    def _():
        b0.start()

    pair_wait(cb, 0)
    c2 = mate_copy(cb, 2)
    c2.start()
    h1.start()

    @pl.when(jnp.logical_and(has_above, r == 0))
    def _():
        b1.start()

    own_c.wait()
    mate_wait(cb, 2)

    def rows_loop(body):
        def run(i, carry):
            i0 = pl.multiple_of(i * rb, rb)
            body(pl.ds(i0, rb), i0)
            return carry

        lax.fori_loop(0, k // rb, run, 0)

    def eye(i0):
        row = lax.broadcasted_iota(jnp.int32, (rb, k), 0) + i0
        col = lax.broadcasted_iota(jnp.int32, (rb, k), 1)
        return row, col

    def base(t, rows, i0):
        row, col = eye(i0)
        out = jnp.where(col == row, energy, 0.0)
        out = jnp.where(col == row + half, -BROAD, out)
        out = jnp.where(col == row - half, BROAD, out)
        return out - hb[t, rows].astype(F32)

    def residue(product, i0):
        row, col = eye(i0)
        return (jnp.where(col == row, 2.0, 0.0) - product).astype(BF)

    def transpose(dst, src):
        for j in range(0, k, 128):
            dst[j:j + 128, :] = src[:, j:j + 128].T

    transpose(ctp, cb[0])
    right[...] = (cb[0].astype(F32) * ge).astype(BF)
    inner[...] = (cb[1].astype(F32) * ge).astype(BF)
    keep = jnp.where(has_above, 1.0, 0.0)

    def first_local(rows, i0):
        mat[0, rows] = dot_nt(cb[0, rows], right[...])
        low = dot_nn(ctp[rows], right[...]).astype(BF).astype(F32)
        mat[1, rows] = keep * dot_nt(cb[1, rows], inner[...]) + low

    rows_loop(first_local)
    pair_wait(hb, 1)
    h2 = mate_copy(hb, 3)
    h2.start()

    @pl.when(has_below)
    def _():
        copy(cbel.at[mine], cbel.at[mine], ini_s.at[4], ini_r.at[4], down_dev).wait_recv()
        b2.start()

    mate_wait(hb, 3)
    own_h.wait()

    def first_end(t, total, rows, i0):
        m = (base(t, rows, i0) - total).astype(BF).astype(F32)
        gb[0, t, rows] = (residue(m * ge, i0).astype(F32) * ge).astype(BF)

    def halo(n, slot):
        down = copy(gb.at[slot, 0], gab.at[n], hal_s.at[n, 0], hal_r.at[n, 0], down_dev)
        up = copy(gb.at[slot, 1], gbe.at[n], hal_s.at[n, 1], hal_r.at[n, 1], up_dev)
        return down, up

    def start_up(n, slot):
        @pl.when(has_above)
        def _():
            halo(n, slot)[1].start()

    def start_down(n, slot):
        @pl.when(has_below)
        def _():
            halo(n, slot)[0].start()

    rows_loop(lambda rows, i0: first_end(1, mat[1, rows], rows, i0))
    start_up(0, 0)

    @pl.when(has_below)
    def _():
        copy(cbel.at[theirs], cbel.at[theirs], ini_s.at[5], ini_r.at[5], (mate, me_s)).wait_recv()

    transpose(ctbel, cbel[...])
    right[...] = (cbel[...].astype(F32) * ge).astype(BF)

    def first_below(rows, i0):
        low = dot_nn(ctbel[rows], right[...]).astype(BF).astype(F32)
        first_end(0, mat[0, rows] + low, rows, i0)

    rows_loop(first_below)
    start_down(0, 0)

    def local_part(n):
        def local_a(rows, i0):
            right[rows] = dot_nt(gb[n, 1, rows], cb[0]).astype(BF)
            inner[rows] = dot_nn(gb[n, 0, rows], cb[0]).astype(BF)

        rows_loop(local_a)

        def local_b(rows, i0):
            mat[0, rows] = base(0, rows, i0) - dot_nn(cb[0, rows], right[...])
            low = dot_nn(ctp[rows], inner[...]).astype(BF).astype(F32)
            mat[1, rows] = base(1, rows, i0) - low

        rows_loop(local_b)

    def remote_part(n, t):
        if t == 1:
            @pl.when(has_above)
            def _():
                copy(gab.at[n], gab.at[n], hal_s.at[n, 0], hal_r.at[n, 0], up_dev).wait_recv()

            def remote_a(rows, i0):
                right[rows] = dot_nt(gab[n, rows], cb[1]).astype(BF)

            rows_loop(remote_a)
            return lambda rows: dot_nn(cb[1, rows], right[...])

        @pl.when(has_below)
        def _():
            copy(gbe.at[n], gbe.at[n], hal_s.at[n, 1], hal_r.at[n, 1], down_dev).wait_recv()

        def remote_b(rows, i0):
            inner[rows] = dot_nn(gbe[n, rows], cbel[...]).astype(BF)

        rows_loop(remote_b)
        return lambda rows: dot_nn(ctbel[rows], inner[...]).astype(BF).astype(F32)

    def finish(n, t, term, last):
        def product(rows, i0):
            m = (mat[t, rows] - term(rows)).astype(BF)
            res[rows] = residue(dot_nn(m, gb[n, t]), i0)

        rows_loop(product)

        def green(rows, i0):
            value = dot_nn(gb[n, t, rows], res[...])
            gb[n + 1, t, rows] = value.astype(BF)
            if last:
                @pl.when(r == t)
                def _():
                    go[t, 0, rows] = value

        rows_loop(green)

    def start_halo(n, t):
        (start_up if t else start_down)(n, n)

    def self_term(t):
        return lambda rows: selfp[t, rows].astype(F32)

    def count(d):
        total = jnp.float32(0.0)
        for j in range(nw):
            total = total + jnp.where(off[j] == d, 1.0 / nw, 0.0)
        return total

    myrows = pl.ds(pl.multiple_of(me_e * rc, rc), rc)

    def scatter(rd, slot, t, method):
        for delta in range(ea):
            oe = lax.rem(me_e + delta, ea)
            rows = pl.ds(pl.multiple_of(oe * rc, rc), rc)
            piece = copy(
                gb.at[slot, t, rows], el.at[rd, flat], a2a_s.at[rd, oe * 2 + t], a2a_r.at[rd, flat],
                (oe, base_s + t),
            )
            if delta == 0:
                pl.when(r != t)(getattr(piece, method))
            else:
                getattr(piece, method)()

    def gather_wait(rd, delta):
        other, oe, orr = peer(delta)
        copy(
            el.at[rd, other], el.at[rd, other], a2a_s.at[rd, other], a2a_r.at[rd, other],
            (oe, base_s + orr),
        ).wait_recv()

    def convolve(rd):
        top = ne // 2
        ahead = [count(d) for d in range(top + 1)]
        behind = [count(-d) for d in range(top + 1)]
        columns = k // 128

        def tile(i, carry):
            rows = pl.ds(pl.multiple_of((i // columns) * 16, 16), 16)
            cols = pl.ds(pl.multiple_of(lax.rem(i, columns) * 128, 128), 128)
            g = [el[rd, e, rows, cols].astype(F32) for e in range(ne)]
            v = vb[rows, cols].astype(F32)
            acc = [jnp.zeros((16, 128), F32) for _ in range(ne)]
            for d in range(top + 1):
                pol = g[0] * g[d]
                for e in range(1, ne - d):
                    pol = pol + g[e] * g[e + d]
                scr = v * (1.0 + (4.0 / ne) * pol * v)
                a = scr * ahead[d]
                b = scr * behind[d]
                for e in range(ne):
                    if e - d >= 0:
                        acc[e] = acc[e] + a * g[e - d]
                    if d > 0 and e + d < ne:
                        acc[e] = acc[e] + b * g[e + d]
            for e in range(ne):
                sf[rd, e, rows, cols] = acc[e].astype(BF)
            return carry

        lax.fori_loop(0, (rc // 16) * columns, tile, 0)

    def gather_all(rd):
        for delta in range(1, ne):
            gather_wait(rd, delta)

    local_part(0)
    for t in (0, 1):
        finish(0, t, remote_part(0, t), False)
        scatter(0, 1, t, "start")
        start_halo(1, t)
    el[0, flat] = gb[1, r, myrows]
    local_part(1)
    own_v.wait()
    gather_all(0)
    convolve(0)

    def back(delta):
        other, oe, orr = peer(delta)
        return copy(
            sf.at[0, other], selfp.at[r, myrows], bk_s.at[0, other], bk_r.at[0, flat],
            (oe, base_s + orr),
        )

    for delta in range(1, ne):
        back(delta).start()
    selfp[r, myrows] = sf[0, flat]
    for t in (0, 1):
        term = remote_part(1, t)

        def add(rows, i0, t=t, term=term):
            mat[t, rows] = mat[t, rows] - term(rows)

        rows_loop(add)
    for delta in range(1, ne):
        other, oe, orr = peer(delta)
        rows = pl.ds(pl.multiple_of(oe * rc, rc), rc)
        copy(
            sf.at[0, other], selfp.at[orr, rows], bk_s.at[0, other], bk_r.at[0, other],
            (oe, base_s + orr),
        ).wait_recv()

    for t in (1, 0):
        finish(1, t, self_term(t), False)
        start_halo(2, t)
    local_part(2)
    for t in (0, 1):
        term = remote_part(2, t)

        def whole(rows, t=t, term=term):
            return selfp[t, rows].astype(F32) + term(rows)

        finish(2, t, whole, True)
        scatter(1, 3, t, "start")
    el[1, flat] = gb[3, r, myrows]
    cross = copy(gb.at[3, 1 - r], gx, gx_s, gx_r, (me_e, partner))
    gather_all(1)
    cross.start()
    convolve(1)

    def home(delta):
        oe = lax.rem(me_e + delta, ea)
        return copy(
            sf.at[1, pl.ds(oe * 2, 2)], ret.at[:, myrows], bk_s.at[1, oe], bk_r.at[1, me_e],
            (oe, me_s),
        )

    for delta in range(1, ea):
        home(delta).start()
    ret[:, myrows] = sf[1, pl.ds(me_e * 2, 2)]
    cross.wait_recv()

    def widen(rows, i0):
        go[1 - r, 0, rows] = gx[rows].astype(F32)

    rows_loop(widen)
    for delta in range(1, ea):
        oe = lax.rem(me_e + delta, ea)
        rows = pl.ds(pl.multiple_of(oe * rc, rc), rc)
        copy(
            sf.at[1, pl.ds(oe * 2, 2)], ret.at[:, rows], bk_s.at[1, oe], bk_r.at[1, oe], (oe, me_s)
        ).wait_recv()
    so[:, 0] = ret[...]

    for c in (c1, h1, c2, h2, cross):
        c.wait_send()

    @pl.when(has_above)
    def _():
        b1.wait_send()
        for n in range(3):
            halo(n, n)[1].wait_send()

    @pl.when(has_below)
    def _():
        b2.wait_send()
        for n in range(3):
            halo(n, n)[0].wait_send()

    for delta in range(1, ne):
        back(delta).wait_send()
    for t in (0, 1):
        scatter(0, 1, t, "wait_send")
        scatter(1, 3, t, "wait_send")
    for delta in range(1, ea):
        home(delta).wait_send()


def local(energies, hamiltonian, coupling, coulomb, offsets):
    k = hamiltonian.shape[1]
    rc = coulomb.shape[1]
    ne = energies.shape[0] * lax.axis_size("energy")
    hbm = pl.BlockSpec(memory_space=pltpu.HBM)
    smem = pl.BlockSpec(memory_space=pltpu.SMEM)
    vmem = pl.BlockSpec(memory_space=pltpu.VMEM)
    dma = pltpu.SemaphoreType.DMA

    def buf(*shape, kind=BF):
        return pltpu.VMEM(shape, kind)

    return pl.pallas_call(
        kernel,
        out_shape=(
            jax.ShapeDtypeStruct((2, 1, k, k), F32),
            jax.ShapeDtypeStruct((2, 1, k, k), BF),
        ),
        in_specs=[smem, smem, hbm, hbm, hbm],
        out_specs=(vmem, vmem),
        scratch_shapes=[
            buf(2, k, k), buf(2, k, k), buf(k, k), buf(k, k), buf(k, k),
            buf(4, 2, k, k), buf(3, k, k), buf(3, k, k), buf(2, k, k),
            buf(2, ne, rc, k), buf(2, ne, rc, k), buf(k, k), buf(2, k, k),
            buf(2, k, k, kind=F32), buf(k, k), buf(k, k), buf(k, k),
            buf(rc, k), dma((3,)),
            dma((6,)), dma((6,)), dma((3, 2)), dma((3, 2)),
            dma((2, ne)), dma((2, ne)), dma((2, ne)), dma((2, ne)), dma, dma,
        ],
        compiler_params=pltpu.CompilerParams(
            collective_id=0, has_side_effects=True, vmem_limit_bytes=60 * 1024 * 1024
        ),
    )(energies, offsets, hamiltonian, coupling, coulomb)


def solution(mesh):
    placed = (
        P("energy"),
        P("slab", None, None),
        P("slab", None, None),
        P("slab", "energy", None),
        P(),
    )
    return jax.shard_map(
        local,
        mesh=mesh,
        in_specs=placed,
        out_specs=(P("energy", "slab", None, None), P("energy", "slab", None, None)),
        check_vma=False,
    )
```
